128 devices in a mesh: row: 16 (over x_lo, y, core), col: 8 (over z, x_hi).
Axes of the slice: x: 4 (x_hi: 2, x_lo: 2; x = x_hi * 2 + x_lo), y: 4, z: 4, core: 2. Of those that a mesh axis runs over, the one named last changes fastest.
Arguments:
- integrals: float32 [4096, 1024], P('row', 'col'), may hold values from -0.1875 to 0.1875
- amplitudes: float32 [10240, 4096], P('row', 'col'), may hold values from -6 to 6
Outputs:
- cycle_residual: float32 [4096, 40960], P('row', 'col')
The draws below stay inside these ranges and needn't reach their ends.
All inputs are finite; a program needn't handle non-finite values.
Results may differ from the reference program's by a relative error of at most 0.00007.
Values sent between devices are 32-bit elements; how exact they have to be, the bound alone decides.
A program may use at most 128 MiB of HBM per device.

```python
import jax
import jax.numpy as jnp
from jax import lax

O = 64
V = 640
KPAIRS = 1024
CW = 16
M = 4096


def level_of(stream_key, dims, cuts, low, largest):
    factor_of, own = 1.0, jax.random.fold_in(stream_key, 6)
    for axis_at, blocks in cuts:
        heights = jnp.exp(jax.random.uniform(jax.random.fold_in(own, axis_at), (blocks,), jnp.float32, low / len(cuts), largest / len(cuts)))
        factor_of = factor_of * jnp.repeat(heights, dims[axis_at] // blocks).reshape([-1 if axis == axis_at else 1 for axis in range(len(dims))])
    return factor_of


def gaussian(key, shape, deviation, bound, split=(), held_as=jnp.bfloat16):
    entries = deviation * jax.random.normal(key, shape, jnp.float32)
    if split:
        entries = entries * level_of(key, shape, split, -0.22, 0.18)
    return jnp.clip(entries, -bound, bound).astype(held_as)


def setup_inputs(seed: int = 0) -> dict:
    key_list = jax.random.split(jax.random.key(seed), 3)
    return {
        "integrals": gaussian(key_list[0], (M, KPAIRS), KPAIRS ** -0.5, 0.1875, ((0, 16), (1, 8)), jnp.float32),
        "amplitudes": gaussian(key_list[1], (CW * V, O * O), 1.0, 6.0, ((0, 16), (1, 8)), jnp.float32),
    }


def reference(integrals, amplitudes):
    blocks = amplitudes.reshape(CW, V, O, O)
    cycle_amplitudes = jnp.transpose(blocks, (0, 2, 1, 3)).reshape(CW * O, V * O)
    return jnp.dot(integrals, cycle_amplitudes, precision=lax.Precision.HIGHEST, preferred_element_type=jnp.float32)
```

```python
import jax
import jax.numpy as jnp
import numpy as np
from jax import lax
from jax.experimental import pallas as pl
from jax.experimental.pallas import tpu as pltpu
from jax.sharding import PartitionSpec as P

MESH = pl.DeviceIdType.MESH
F32, BF16 = jnp.float32, jnp.bfloat16
O, V, K = 64, 640, 1024
COLS = 5120
CHUNKS = 8
W = COLS // CHUNKS
W4 = 256
W1 = W - W4
GROUPS = COLS // 512


def cols_of(n, first=0, width=W):
    return pl.ds(pl.multiple_of(n * W + first, 128), width)


def rows_of(start, count):
    return pl.ds(pl.multiple_of(start, 8), count)


def regroup(x_ref, tmp, stage, groups):
    low = lax.broadcasted_iota(jnp.int32, (8, 128), 1) < 64

    @pl.loop(0, 8)
    def _(q):
        for slot, g in enumerate(groups):
            for t in range(4):
                v = x_ref[rows_of(q * 80 + g * 8, 8), t * 128 : (t + 1) * 128]
                nxt = pltpu.roll(v, 7, 0)
                tmp[slot, 2 * t] = jnp.where(low, v, pltpu.roll(nxt, 64, 1))
                tmp[slot, 2 * t + 1] = jnp.where(low, pltpu.roll(v, 64, 1), nxt)
            for u in range(4):
                at = (g * 4 + u) * 128
                stage[rows_of(q * 8, 8), at : at + 128] = tmp[slot, :, 2 * u, :]


def kernel(a_ref, x_ref, perm_ref, o_ref, b, stage, tmp, ag, al, c_buf,
           p1, in1, t4y, t1y, t4f, t1f, in4, sib, asem, ssem, assem, csem, osem):
    r, q = lax.axis_index("row"), lax.axis_index("col")
    xlo, y, core = r // 8, (r // 2) % 4, r % 2
    z, xhi = q // 2, q % 2
    side = (xlo + xhi) % 2

    def dev(xlo, y, core, z, xhi):
        return (xlo * 8 + y * 2 + core, z * 2 + xhi)

    def block(y):
        return core * 512 + y * 128

    yp, ym, y2 = (y + 1) % 4, (y + 3) % 4, (y + 2) % 4
    up, down = dev(xlo, yp, core, z, xhi), dev(xlo, ym, core, z, xhi)
    inner = dev(1 - xlo, y, core, z, xhi)
    sibling = dev(xlo, y, 1 - core, z, xhi)
    far = dev(xlo, y, core, z, 1 - xhi)
    mates = []
    for dz in range(4):
        for dx in range(2):
            if dz or dx:
                oz, ox = (z + dz) % 4, (xhi + dx) % 2
                mates.append((oz * 2 + ox, dev((side + ox) % 2, y, core, oz, ox)))
    zmates = [dev(xlo, y, core, (z + d) % 4, xhi) for d in (1, 2, 3)]
    mine = block(y) + side * 64
    other = (1 - side) * 64

    barrier = pltpu.get_barrier_semaphore()
    greeted = [m for _, m in mates] + [up, down, inner, sibling, far]
    for d in greeted:
        pl.semaphore_signal(barrier, inc=1, device_id=d, device_id_type=MESH)
    regroup(x_ref, tmp, stage, (0, 1))
    pl.semaphore_wait(barrier, len(greeted))

    def push(n, row, count, cols, to, recv):
        ref = b.at[rows_of(row, count), cols]
        pltpu.make_async_remote_copy(
            src_ref=ref, dst_ref=ref, send_sem=ssem.at[n], recv_sem=recv, device_id=to, device_id_type=MESH
        ).start()

    def arrived(row, count, cols, recv):
        ref = b.at[rows_of(row, count), cols]
        pltpu.make_async_copy(ref, ref, recv).wait()

    def exchange(n):
        for oq, d in mates:
            pltpu.make_async_remote_copy(
                src_ref=stage.at[rows_of(oq * 8, 8), cols_of(n)],
                dst_ref=b.at[rows_of(mine + q * 8, 8), cols_of(n)],
                send_sem=ssem.at[n], recv_sem=p1.at[n], device_id=d, device_id_type=MESH,
            ).start()

    def a_push(src, slot, to, i):
        return pltpu.make_async_remote_copy(
            src_ref=src, dst_ref=ag.at[slot], send_sem=assem.at[i], recv_sem=asem.at[i],
            device_id=to, device_id_type=MESH,
        )

    fq = z * 2 + 1 - xhi

    def a_copies():
        first = [a_push(a_ref, q, far, 0)] + [a_push(a_ref, q, d, 1 + i) for i, d in enumerate(zmates)]
        second = [a_push(ag.at[fq], fq, d, 4 + i) for i, d in enumerate(zmates)]
        return first, second

    def a_arrived(slot, i):
        pltpu.make_async_copy(ag.at[slot], ag.at[slot], asem.at[i]).wait()

    exchange(0)
    regroup(x_ref, tmp, stage, (2, 3, 4))
    exchange(1)
    own = pltpu.make_async_copy(stage.at[rows_of(q * 8, 8)], b.at[rows_of(mine + q * 8, 8)], osem)
    regroup(x_ref, tmp, stage, (5, 6, 7, 8, 9))
    own.start()
    own.wait()

    @pl.loop(0, CHUNKS + 4)
    def _(i):
        @pl.when(i < CHUNKS)
        def _():
            n = i
            c4, c1 = cols_of(n, 0, W4), cols_of(n, W4, W1)
            arrived(0, 56, cols_of(n), p1.at[n])
            push(n, mine, 64, c1, inner, in1.at[n])
            push(n, mine, 64, c4, up, t4y.at[n, 0])
            push(n, mine, 64, c4, down, t4y.at[n, 1])
            push(n, mine, 64, c4, inner, in4.at[n, 0])

        @pl.when(i < CHUNKS - 2)
        def _():
            exchange(i + 2)

        @pl.when(i == 0)
        def _():
            for c in a_copies()[0]:
                c.start()

        @pl.when(jnp.logical_and(i >= 1, i < CHUNKS + 1))
        def _():
            n = i - 1
            c4, c1 = cols_of(n, 0, W4), cols_of(n, W4, W1)
            arrived(block(y) + other, 64, c1, in1.at[n])
            push(n, block(y), 128, c1, up, t1y.at[n, 0])
            push(n, block(y), 128, c1, down, t1y.at[n, 1])
            arrived(block(ym) + side * 64, 64, c4, t4y.at[n, 0])
            push(n, block(ym) + side * 64, 32, c4, up, t4f.at[n, 0])
            push(n, block(ym) + side * 64, 64, c4, inner, in4.at[n, 1])
            arrived(block(yp) + side * 64, 64, c4, t4y.at[n, 1])
            push(n, block(yp) + side * 64 + 32, 32, c4, down, t4f.at[n, 1])
            push(n, block(yp) + side * 64, 64, c4, inner, in4.at[n, 2])

        @pl.when(i == 1)
        def _():
            a_arrived(fq, 0)
            for c in a_copies()[1]:
                c.start()

        @pl.when(jnp.logical_and(i >= 2, i < CHUNKS + 2))
        def _():
            n = i - 2
            c4, c1 = cols_of(n, 0, W4), cols_of(n, W4, W1)
            arrived(block(ym), 128, c1, t1y.at[n, 0])
            push(n, block(ym), 64, c1, up, t1f.at[n, 0])
            arrived(block(yp), 128, c1, t1y.at[n, 1])
            push(n, block(yp) + 64, 64, c1, down, t1f.at[n, 1])
            arrived(block(y2) + side * 64, 32, c4, t4f.at[n, 0])
            arrived(block(y2) + side * 64 + 32, 32, c4, t4f.at[n, 1])
            push(n, block(y2) + side * 64, 64, c4, inner, in4.at[n, 3])
            for j, yy in enumerate((y, ym, yp)):
                arrived(block(yy) + other, 64, c4, in4.at[n, j])
                push(n, block(yy), 128, cols_of(n), sibling, sib.at[n, j])

        @pl.when(jnp.logical_and(i >= 3, i < CHUNKS + 3))
        def _():
            n = i - 3
            c4, c1 = cols_of(n, 0, W4), cols_of(n, W4, W1)
            arrived(block(y2), 64, c1, t1f.at[n, 0])
            arrived(block(y2) + 64, 64, c1, t1f.at[n, 1])
            arrived(block(y2) + other, 64, c4, in4.at[n, 3])
            push(n, block(y2), 128, cols_of(n), sibling, sib.at[n, 3])

        @pl.when(i == 3)
        def _():
            for j in range(3):
                d = 3 - j
                a_arrived(((z + d) % 4) * 2 + xhi, 1 + j)
                a_arrived(((z + d) % 4) * 2 + 1 - xhi, 4 + j)
            ag[q] = a_ref[...]
            for yy in range(4):
                t = jnp.concatenate([ag[yy], ag[4 + yy]], axis=1)
                hi = t.astype(BF16)
                lo = (t - hi.astype(F32)).astype(BF16)
                both = jnp.dot(jnp.concatenate([hi, lo], axis=0), perm_ref[...], preferred_element_type=F32)
                both = both.astype(BF16)
                for c in range(2):
                    al[:, c * 512 + yy * 128 : c * 512 + yy * 128 + 128] = both[:, c * 128 : c * 128 + 128]

        @pl.when(i >= 4)
        def _():
            n = i - 4
            for j, yy in enumerate((y, ym, yp, y2)):
                arrived((1 - core) * 512 + yy * 128, 128, cols_of(n), sib.at[n, j])
            for at, width in ((0, 256), (256, 256), (512, 128)):
                t = b[:, cols_of(n, at, width)]
                hi = t.astype(BF16)
                lo = (t - hi.astype(F32)).astype(BF16)
                one = jnp.dot(al[...], hi, preferred_element_type=F32)
                two = jnp.dot(al[0:256], lo, preferred_element_type=F32)
                c_buf[:, cols_of(n, at, width)] = one[0:256] + (one[256:512] + two)
            pltpu.make_async_copy(c_buf.at[:, cols_of(n)], o_ref.at[:, cols_of(n)], csem.at[n]).start()

    @pl.loop(0, CHUNKS)
    def _(n):
        pltpu.make_async_copy(c_buf.at[:, cols_of(n)], o_ref.at[:, cols_of(n)], csem.at[n]).wait()
        sent = b.at[0:1016, cols_of(n)]
        pltpu.make_async_copy(sent, sent, ssem.at[n]).wait()

    for group in a_copies():
        for c in group:
            c.wait_send()


def permutation():
    perm = np.zeros((256, 256), np.float32)
    for o in range(256):
        core, side, s, k8 = o // 128, (o // 64) % 2, (o // 8) % 8, o % 8
        perm[((side + s) % 2) * 128 + core * 64 + s * 8 + k8, o] = 1
    return perm


def per_device(integrals, amplitudes):
    vmem = pl.BlockSpec(memory_space=pltpu.VMEM)
    dma = pltpu.SemaphoreType.DMA
    return pl.pallas_call(
        kernel,
        name="cycle",
        out_shape=jax.ShapeDtypeStruct((256, COLS), F32),
        in_specs=[vmem, vmem, vmem],
        out_specs=pl.BlockSpec(memory_space=pl.ANY),
        scratch_shapes=[
            pltpu.VMEM((K, COLS), F32),
            pltpu.VMEM((64, COLS), F32),
            pltpu.VMEM((5, 8, 8, 128), F32),
            pltpu.VMEM((8, 256, 128), F32),
            pltpu.VMEM((512, K), BF16),
            pltpu.VMEM((256, COLS), F32),
            dma((CHUNKS,)),
            dma((CHUNKS,)),
            dma((CHUNKS, 2)),
            dma((CHUNKS, 2)),
            dma((CHUNKS, 2)),
            dma((CHUNKS, 2)),
            dma((CHUNKS, 4)),
            dma((CHUNKS, 4)),
            dma((7,)),
            dma((CHUNKS,)),
            dma((7,)),
            dma((CHUNKS,)),
            dma(()),
        ],
        compiler_params=pltpu.CompilerParams(collective_id=0, has_side_effects=True, vmem_limit_bytes=50 << 20),
        cost_estimate=pl.CostEstimate(flops=3 * 2 * 256 * K * COLS, bytes_accessed=7 << 20, transcendentals=0),
    )(integrals, amplitudes, jnp.asarray(permutation(), BF16))


def solution(mesh):
    placed = (P("row", "col"), P("row", "col"))
    return jax.shard_map(
        per_device, mesh=mesh, in_specs=placed, out_specs=P("row", "col"), check_vma=False
    )
```

```python
import jax
import jax.numpy as jnp
from jax import lax
from jax.experimental import pallas as pl
from jax.experimental.pallas import tpu as pltpu
from jax.sharding import PartitionSpec as P

MESH = pl.DeviceIdType.MESH
F32, BF16 = jnp.float32, jnp.bfloat16
COLS = 5120
W = 256
PAIRED = 6
FULL = (COLS - 2 * PAIRED * W) // W
N = PAIRED + FULL
HALF = PAIRED * W
GROUPS = ((0, 1, -2), (1, 2, -1), (3, 3, 0), (6, 4, 4), (10, 4, 7))
A_PAIR, A_OWN, A_NEXT = 2, 5, 2
LAG2, LAG3, LAGC, LAGO = 2, 4, 6, 9


def at(start, size, unit):
    return pl.ds(pl.multiple_of(start, unit), size)


def regroup(x_ref, tmp, stage, groups):
    low = lax.broadcasted_iota(jnp.int32, (8, 128), 1) < 64

    @pl.loop(0, 8)
    def _(q):
        for slot, g in enumerate(groups):
            for t in range(4):
                v = x_ref[at(q * 80 + g * 8, 8, 8), t * 128 : (t + 1) * 128]
                nxt = pltpu.roll(v, 7, 0)
                tmp[slot, 2 * t] = jnp.where(low, v, pltpu.roll(nxt, 64, 1))
                tmp[slot, 2 * t + 1] = jnp.where(low, pltpu.roll(v, 64, 1), nxt)
            for u in range(4):
                col = (g * 4 + u) * 128
                stage[at(q * 8, 8, 8), col : col + 128] = tmp[slot, :, 2 * u, :]


def permutation(xlo, z, xhi):
    i = lax.broadcasted_iota(jnp.int32, (256, 256), 0)
    o = lax.broadcasted_iota(jnp.int32, (256, 256), 1)
    from_xlo = (xlo + (o >> 6)) & 1
    from_z = (z + 4 - ((o >> 4) & 3)) & 3
    from_xhi = (xhi + (o >> 3)) & 1
    source = from_xlo * 128 + ((o >> 7) & 1) * 64 + from_z * 16 + from_xhi * 8 + (o & 7)
    return (i == source).astype(F32).astype(BF16)


def kernel(a_in, x_in, o_ref, b, stage, tmp, ag, al, c_out, x_ref,
           ex, exs, ty, tf, sib, cr, ssem, cs, ar, asend, lsem):
    r, q = lax.axis_index("row"), lax.axis_index("col")
    xlo, y, core = r // 8, (r // 2) % 4, r % 2
    z, xhi = q // 2, q % 2

    def dev(xlo, y, core, z, xhi):
        return (xlo * 8 + y * 2 + core, z * 2 + xhi)

    up, down = dev(xlo, (y + 1) % 4, core, z, xhi), dev(xlo, (y + 3) % 4, core, z, xhi)
    inner = dev(1 - xlo, y, core, z, xhi)
    outer = dev(1 - xlo, y, core, z, 1 - xhi)
    sibling = dev(xlo, y, 1 - core, z, xhi)
    plane = []
    for d in range(1, 16):
        oxlo, oz, oxhi = (xlo + d // 8) % 2, (z + (d // 2) % 4) % 4, (xhi + d % 2) % 2
        plane.append((d, oxlo, oz * 2 + oxhi, dev(oxlo, y, core, oz, oxhi)))
    z_up, z_down = dev(xlo, y, core, (z + 1) % 4, xhi), dev(xlo, y, core, (z + 3) % 4, xhi)

    load_x = pltpu.make_async_copy(x_in, x_ref, lsem.at[0])
    load_a = pltpu.make_async_copy(a_in, ag.at[0, q], lsem.at[1])
    load_x.start()
    load_a.start()
    barrier = pltpu.get_barrier_semaphore()
    greeted = [p[3] for p in plane] + [up, down, sibling]
    for d in greeted:
        pl.semaphore_signal(barrier, inc=1, device_id=d, device_id_type=MESH)
    load_x.wait()
    regroup(x_ref, tmp, stage, (0, HALF // 512))
    pl.semaphore_wait(barrier, len(greeted))

    def cols(n):
        return at(n * W, W, W)

    def push(n, src, dst, count, to, recv):
        pltpu.make_async_remote_copy(
            src_ref=b.at[at(src, count, 8), cols(n)], dst_ref=b.at[at(dst, count, 8), cols(n)],
            send_sem=ssem.at[n], recv_sem=recv, device_id=to, device_id_type=MESH,
        ).start()

    def arrived(n, row, count, recv):
        ref = b.at[at(row, count, 8), cols(n)]
        pltpu.make_async_copy(ref, ref, recv).wait()

    def mine(slot):
        return slot * 256 + core * 128

    def exchange(g):
        n, count, _ = GROUPS[g]
        for d, oxlo, oq, to in plane:
            first = at(oxlo * HALF + n * W, count * W, W) if n < PAIRED else pl.ds(HALF + n * W, count * W)
            pltpu.make_async_remote_copy(
                src_ref=stage.at[at(oq * 8, 8, 8), first],
                dst_ref=b.at[at(mine(0) + d * 8, 8, 8), pl.ds(n * W, count * W)],
                send_sem=exs.at[g], recv_sem=ex.at[g], device_id=to, device_id_type=MESH,
            ).start()

    def exchanged(g, sem):
        n, count, _ = GROUPS[g]
        ref = b.at[at(mine(0) + 8, 120, 8), pl.ds(n * W, count * W)]
        pltpu.make_async_copy(ref, ref, sem.at[g]).wait()

    def own_piece():
        rows, into = at(q * 8, 8, 8), at(mine(0), 8, 8)
        return [
            pltpu.make_async_copy(stage.at[rows, at(xlo * HALF, HALF, W)], b.at[into, 0:HALF], lsem.at[2]),
            pltpu.make_async_copy(stage.at[rows, 2 * HALF : COLS], b.at[into, HALF : N * W], lsem.at[3]),
        ]

    def a_push(rows, block, to_rows, i, to, part=pl.ds(0, 256)):
        return pltpu.make_async_remote_copy(
            src_ref=ag.at[rows, block, part], dst_ref=ag.at[to_rows, block, part],
            send_sem=asend.at[i], recv_sem=ar.at[i], device_id=to, device_id_type=MESH,
        )

    def a_arrived(rows, block, i, part=pl.ds(0, 256)):
        ref = ag.at[rows, block, part]
        pltpu.make_async_copy(ref, ref, ar.at[i]).wait()

    qo = z * 2 + 1 - xhi
    a_x = lambda: [a_push(0, q, 1, 0, inner), a_push(0, q, 1, 1, outer)]
    a_far = lambda: [a_push(1, q, 0, 2, outer)]
    top, bottom = pl.ds(0, 128), pl.ds(128, 128)

    def a_block(step, j):
        return ((z + step) % 4) * 2 + (xhi if j == 0 else 1 - xhi)

    def a_z(rows, i):
        return [
            a_push(rows, a_block(0, j), rows, i + 2 * j + k, to) for j in range(2) for k, to in enumerate((z_up, z_down))
        ]

    def a_z_next(rows, i):
        return [
            a_push(rows, a_block(3, j), rows, i + 4 + 2 * j, z_up, top) for j in range(2)
        ] + [
            a_push(rows, a_block(1, j), rows, i + 5 + 2 * j, z_down, bottom) for j in range(2)
        ]

    def a_z_arrived(rows, i):
        for j in range(2):
            a_arrived(rows, a_block(3, j), i + 2 * j)
            a_arrived(rows, a_block(1, j), i + 2 * j + 1)

    def a_z_all(rows, i):
        for j in range(2):
            a_arrived(rows, a_block(2, j), i + 4 + 2 * j, top)
            a_arrived(rows, a_block(2, j), i + 5 + 2 * j, bottom)

    def a_split(rows):
        perm = permutation(xlo, z, xhi)
        for slot, step in enumerate((0, 3, 1, 2)):
            yy = (y + step) % 4
            t = jnp.concatenate([ag[rows, yy], ag[rows, 4 + yy]], axis=1)
            hi = t.astype(BF16)
            lo = (t - hi.astype(F32)).astype(BF16)
            both = jnp.dot(jnp.concatenate([hi, lo], axis=0), perm, preferred_element_type=F32)
            al[rows, :, slot * 256 : slot * 256 + 256] = both.astype(BF16)

    def product(rows, n, first, depth):
        t = b[first : first + depth, cols(n)]
        hi = t.astype(BF16)
        lo = (t - hi.astype(F32)).astype(BF16)
        one = jnp.dot(al[rows, :, first : first + depth], hi, preferred_element_type=F32)
        two = jnp.dot(al[rows, 0:256, first : first + depth], lo, preferred_element_type=F32)
        return one[0:256] + (one[256:512] + two)

    def all_here(n, slots):
        for slot in slots:
            arrived(n, slot * 256 + (1 - core) * 128, 128, sib.at[n, slot])

    def c_copy(n):
        return pltpu.make_async_remote_copy(
            src_ref=c_out.at[n], dst_ref=o_ref.at[:, at(xlo * HALF + n * W, W, W)],
            send_sem=cs.at[n], recv_sem=cr.at[n], device_id=inner, device_id_type=MESH,
        )

    exchange(0)
    load_a.wait()
    for c in a_x():
        c.start()
    regroup(x_ref, tmp, stage, (1, 2, HALF // 512 + 1, HALF // 512 + 2))
    exchange(1)
    regroup(x_ref, tmp, stage, tuple(range(2 * HALF // 512, COLS // 512)))
    pieces = own_piece()
    for c in pieces:
        c.start()
    for c in pieces:
        c.wait()

    def when(*conditions):
        ok = conditions[0]
        for c in conditions[1:]:
            ok = jnp.logical_and(ok, c)
        return pl.when(ok)

    @pl.loop(0, N + LAGC)
    def _(i):
        for g, (first, _, start) in enumerate(GROUPS):
            if start >= 0:
                @when(i == start)
                def _(g=g):
                    exchange(g)

            @when(i == first)
            def _(g=g):
                exchanged(g, ex)

        @when(i < N)
        def _():
            n = i
            push(n, mine(0), 256 + core * 128, 128, up, ty.at[n, 0])
            push(n, mine(0), 512 + core * 128, 128, down, ty.at[n, 1])

        @when(i == A_PAIR)
        def _():
            a_arrived(1, q, 0)
            a_arrived(1, qo, 1)
            for c in a_z(1, 3) + a_far():
                c.start()

        @when(i == A_OWN)
        def _():
            a_arrived(0, qo, 2)
            for c in a_z(0, 11):
                c.start()

        @when(i == A_PAIR + A_NEXT)
        def _():
            a_z_arrived(1, 3)
            for c in a_z_next(1, 3):
                c.start()

        @when(i == A_OWN + A_NEXT)
        def _():
            a_z_arrived(0, 11)
            for c in a_z_next(0, 11):
                c.start()

        @when(i >= LAG2, i < N + LAG2)
        def _():
            n = i - LAG2
            arrived(n, mine(1), 128, ty.at[n, 0])
            push(n, mine(1), mine(3), 64, up, tf.at[n, 0])
            arrived(n, mine(2), 128, ty.at[n, 1])
            push(n, mine(2) + 64, mine(3) + 64, 64, down, tf.at[n, 1])
            for slot in range(3):
                push(n, mine(slot), mine(slot), 128, sibling, sib.at[n, slot])

        @when(i >= LAG3, i < N + LAG3)
        def _():
            n = i - LAG3
            arrived(n, mine(3), 64, tf.at[n, 0])
            arrived(n, mine(3) + 64, 64, tf.at[n, 1])
            push(n, mine(3), mine(3), 128, sibling, sib.at[n, 3])

        @when(i == LAGC)
        def _():
            a_z_all(1, 3)
            a_split(1)

        @when(i >= LAGC, i < LAGC + PAIRED)
        def _():
            n = i - LAGC
            all_here(n, range(4))
            c_out[n] = product(1, n, 0, 1024)
            c_copy(n).start()

        @when(i == LAGO)
        def _():
            a_z_all(0, 11)
            a_split(0)

        @when(i >= LAGO, i < LAGO + PAIRED)
        def _():
            n = i - LAGO
            o_ref[:, at(xlo * HALF + n * W, W, W)] = product(0, n, 0, 1024)

        @when(i >= LAGC + PAIRED)
        def _():
            n = i - LAGC
            all_here(n, range(3))
            part = product(0, n, 0, 768)
            all_here(n, (3,))
            o_ref[:, at(HALF + n * W, W, W)] = part + product(0, n, 768, 256)

    @pl.loop(0, PAIRED)
    def _(n):
        c = pltpu.make_async_copy(c_out.at[n], o_ref.at[:, at((1 - xlo) * HALF + n * W, W, W)], cr.at[n])
        c.wait()
        pltpu.make_async_copy(c_out.at[n], c_out.at[n], cs.at[n]).wait()

    @pl.loop(0, N)
    def _(n):
        sent = b.at[0:896, cols(n)]
        pltpu.make_async_copy(sent, sent, ssem.at[n]).wait()

    for g in range(len(GROUPS)):
        exchanged(g, exs)
    for c in a_x() + a_far() + a_z(1, 3) + a_z(0, 11) + a_z_next(1, 3) + a_z_next(0, 11):
        c.wait_send()


def write(c_ref, o_ref, sem):
    parts = [(c_ref.at[pl.ds(32 * i, 32)], o_ref.at[pl.ds(32 * i, 32)], sem.at[i]) for i in range(8)]
    for part in parts:
        pltpu.make_async_copy(*part).start()
    for part in parts:
        pltpu.make_async_copy(*part).wait()


def per_device(integrals, amplitudes):
    dma = pltpu.SemaphoreType.DMA
    anywhere = pl.BlockSpec(memory_space=pl.ANY)
    c = pl.pallas_call(
        kernel,
        name="cycle",
        out_shape=pltpu.VMEM((256, COLS), F32),
        in_specs=[anywhere, anywhere],
        out_specs=pl.BlockSpec(memory_space=pltpu.VMEM),
        scratch_shapes=[
            pltpu.VMEM((1024, N * W), F32),
            pltpu.VMEM((64, COLS), F32),
            pltpu.VMEM((4, 8, 8, 128), F32),
            pltpu.VMEM((2, 8, 256, 128), F32),
            pltpu.VMEM((2, 512, 1024), BF16),
            pltpu.VMEM((PAIRED, 256, W), F32),
            pltpu.VMEM((640, 512), F32),
            dma((len(GROUPS),)),
            dma((len(GROUPS),)),
            dma((N, 2)),
            dma((N, 2)),
            dma((N, 4)),
            dma((PAIRED,)),
            dma((N,)),
            dma((PAIRED,)),
            dma((19,)),
            dma((19,)),
            dma((4,)),
        ],
        compiler_params=pltpu.CompilerParams(collective_id=0, has_side_effects=True, vmem_limit_bytes=52 << 20),
        cost_estimate=pl.CostEstimate(flops=3 * 2 * 256 * 1024 * COLS, bytes_accessed=7 << 20, transcendentals=0),
    )(integrals, amplitudes)
    return pl.pallas_call(
        write,
        name="write",
        out_shape=jax.ShapeDtypeStruct((256, COLS), F32),
        in_specs=[pl.BlockSpec(memory_space=pltpu.VMEM)],
        out_specs=anywhere,
        scratch_shapes=[dma((8,))],
        compiler_params=pltpu.CompilerParams(vmem_limit_bytes=8 << 20),
    )(c)


def solution(mesh):
    placed = (P("row", "col"), P("row", "col"))
    return jax.shard_map(
        per_device, mesh=mesh, in_specs=placed, out_specs=P("row", "col"), check_vma=False
    )
```

```python
import jax
import jax.numpy as jnp
from jax import lax
from jax.experimental import pallas as pl
from jax.experimental.pallas import tpu as pltpu
from jax.sharding import PartitionSpec as P

MESH = pl.DeviceIdType.MESH
F32, BF16 = jnp.float32, jnp.bfloat16
COLS = 5120
W = 256
PAIRED = 6
FULL = (COLS - 2 * PAIRED * W) // W
N = PAIRED + FULL
HALF = PAIRED * W
GROUPS = ((0, 1, -2), (1, 2, -1), (3, 3, 0), (6, 4, 4), (10, 4, 7))
A_PAIR, A_OWN, A_NEXT = 2, 5, 2
LAG2, LAG3, LAGC, LAGO = 2, 4, 6, 9


def at(start, size, unit):
    return pl.ds(pl.multiple_of(start, unit), size)


def load(x_in, x_ref, lsem, g):
    rows = pl.ds(g * 8, 8)
    return pltpu.make_async_copy(x_in.at[:, rows], x_ref.at[:, rows], lsem.at[g])


def regroup(x_in, x_ref, lsem, tmp, stage, groups, first_q=0, count=8, wait=True):
    low = lax.broadcasted_iota(jnp.int32, (8, 128), 1) < 64
    for g in groups if wait else ():
        load(x_in, x_ref, lsem, g).wait()

    @pl.loop(0, count)
    def _(i):
        q = (first_q + i) % 8
        for slot, g in enumerate(groups):
            for t in range(4):
                v = x_ref[q, g * 8 : g * 8 + 8, t * 128 : (t + 1) * 128]
                nxt = pltpu.roll(v, 7, 0)
                tmp[slot, 2 * t] = jnp.where(low, v, pltpu.roll(nxt, 64, 1))
                tmp[slot, 2 * t + 1] = jnp.where(low, pltpu.roll(v, 64, 1), nxt)
            for u in range(4):
                col = (g * 4 + u) * 128
                stage[at(q * 8, 8, 8), col : col + 128] = tmp[slot, :, 2 * u, :]


def permutation(xlo, z, xhi):
    i = lax.broadcasted_iota(jnp.int32, (256, 256), 0)
    o = lax.broadcasted_iota(jnp.int32, (256, 256), 1)
    from_xlo = (xlo + (o >> 6)) & 1
    from_z = (z + 4 - ((o >> 4) & 3)) & 3
    from_xhi = (xhi + (o >> 3)) & 1
    source = from_xlo * 128 + ((o >> 7) & 1) * 64 + from_z * 16 + from_xhi * 8 + (o & 7)
    return (i == source).astype(F32).astype(BF16)


def kernel(a_in, x_in, o_ref, b, stage, tmp, ag, al, c_out, x_ref,
           ex, exs, ty, tf, sib, cr, ssem, cs, ar, asend, lsem, oy, oys):
    r, q = lax.axis_index("row"), lax.axis_index("col")
    xlo, y, core = r // 8, (r // 2) % 4, r % 2
    z, xhi = q // 2, q % 2

    def dev(xlo, y, core, z, xhi):
        return (xlo * 8 + y * 2 + core, z * 2 + xhi)

    up, down = dev(xlo, (y + 1) % 4, core, z, xhi), dev(xlo, (y + 3) % 4, core, z, xhi)
    inner = dev(1 - xlo, y, core, z, xhi)
    outer = dev(1 - xlo, y, core, z, 1 - xhi)
    sibling = dev(xlo, y, 1 - core, z, xhi)
    plane = []
    for d in range(1, 16):
        oxlo, oz, oxhi = (xlo + d // 8) % 2, (z + (d // 2) % 4) % 4, (xhi + d % 2) % 2
        plane.append((d, oxlo, oz * 2 + oxhi, dev(oxlo, y, core, oz, oxhi)))
    z_up, z_down = dev(xlo, y, core, (z + 1) % 4, xhi), dev(xlo, y, core, (z + 3) % 4, xhi)

    first = (0, HALF // 512)
    rest = tuple(g for g in range(COLS // 512) if g not in first)
    for g in first + rest:
        load(x_in, x_ref, lsem, g).start()
    load_a = pltpu.make_async_copy(a_in, ag.at[0, q], lsem.at[10])
    load_a.start()
    barrier = pltpu.get_barrier_semaphore()
    greeted = [p[3] for p in plane] + [up, down, sibling]
    for d in greeted:
        pl.semaphore_signal(barrier, inc=1, device_id=d, device_id_type=MESH)
    regroup(x_in, x_ref, lsem, tmp, stage, first)
    pl.semaphore_wait(barrier, len(greeted))

    def cols(n):
        return at(n * W, W, W)

    def push(n, src, dst, count, to, recv):
        pltpu.make_async_remote_copy(
            src_ref=b.at[at(src, count, 8), cols(n)], dst_ref=b.at[at(dst, count, 8), cols(n)],
            send_sem=ssem.at[n], recv_sem=recv, device_id=to, device_id_type=MESH,
        ).start()

    def arrived(n, row, count, recv):
        ref = b.at[at(row, count, 8), cols(n)]
        pltpu.make_async_copy(ref, ref, recv).wait()

    def mine(slot):
        return slot * 256 + core * 128

    def exchange(g):
        n, count, _ = GROUPS[g]
        for d, oxlo, oq, to in plane:
            first = at(oxlo * HALF + n * W, count * W, W) if n < PAIRED else pl.ds(HALF + n * W, count * W)
            pltpu.make_async_remote_copy(
                src_ref=stage.at[at(oq * 8, 8, 8), first],
                dst_ref=b.at[at(mine(0) + d * 8, 8, 8), pl.ds(n * W, count * W)],
                send_sem=exs.at[g], recv_sem=ex.at[g], device_id=to, device_id_type=MESH,
            ).start()

    def exchanged(g, sem):
        n, count, _ = GROUPS[g]
        ref = b.at[at(mine(0) + 8, 120, 8), pl.ds(n * W, count * W)]
        pltpu.make_async_copy(ref, ref, sem.at[g]).wait()

    parts = ((at(xlo * HALF, HALF, 128), pl.ds(0, HALF)), (pl.ds(2 * HALF, FULL * W), pl.ds(HALF, FULL * W)))

    def own_piece():
        src = at(q * 8, 8, 8)
        return [
            pltpu.make_async_copy(stage.at[src, frm], b.at[at(mine(0), 8, 8), to], lsem.at[11 + j])
            for j, (frm, to) in enumerate(parts)
        ]

    def own_along_y():
        src = at(q * 8, 8, 8)
        return [
            pltpu.make_async_remote_copy(
                src_ref=stage.at[src, frm], dst_ref=b.at[at(mine(1 + k), 8, 8), to],
                send_sem=oys.at[2 * j + k], recv_sem=oy.at[2 * j + k], device_id=d, device_id_type=MESH,
            )
            for j, (frm, to) in enumerate(parts) for k, d in enumerate((up, down))
        ]

    def own_arrived():
        for j, (_, to) in enumerate(parts):
            for k in range(2):
                ref = b.at[at(mine(1 + k), 8, 8), to]
                pltpu.make_async_copy(ref, ref, oy.at[2 * j + k]).wait()

    def a_push(rows, block, to_rows, i, to, part=pl.ds(0, 256)):
        return pltpu.make_async_remote_copy(
            src_ref=ag.at[rows, block, part], dst_ref=ag.at[to_rows, block, part],
            send_sem=asend.at[i], recv_sem=ar.at[i], device_id=to, device_id_type=MESH,
        )

    def a_arrived(rows, block, i, part=pl.ds(0, 256)):
        ref = ag.at[rows, block, part]
        pltpu.make_async_copy(ref, ref, ar.at[i]).wait()

    qo = z * 2 + 1 - xhi
    a_x = lambda: [a_push(0, q, 1, 0, inner), a_push(0, q, 1, 1, outer)]
    a_far = lambda: [a_push(1, q, 0, 2, outer)]
    top, bottom = pl.ds(0, 128), pl.ds(128, 128)

    def a_block(step, j):
        return ((z + step) % 4) * 2 + (xhi if j == 0 else 1 - xhi)

    def a_z(rows, i):
        return [
            a_push(rows, a_block(0, j), rows, i + 2 * j + k, to) for j in range(2) for k, to in enumerate((z_up, z_down))
        ]

    def a_z_next(rows, i):
        return [
            a_push(rows, a_block(3, j), rows, i + 4 + 2 * j, z_up, top) for j in range(2)
        ] + [
            a_push(rows, a_block(1, j), rows, i + 5 + 2 * j, z_down, bottom) for j in range(2)
        ]

    def a_z_arrived(rows, i):
        for j in range(2):
            a_arrived(rows, a_block(3, j), i + 2 * j)
            a_arrived(rows, a_block(1, j), i + 2 * j + 1)

    def a_z_all(rows, i):
        for j in range(2):
            a_arrived(rows, a_block(2, j), i + 4 + 2 * j, top)
            a_arrived(rows, a_block(2, j), i + 5 + 2 * j, bottom)

    def a_split(rows):
        perm = permutation(xlo, z, xhi)
        for slot, step in enumerate((0, 3, 1, 2)):
            yy = (y + step) % 4
            t = jnp.concatenate([ag[rows, yy], ag[rows, 4 + yy]], axis=1)
            hi = t.astype(BF16)
            lo = (t - hi.astype(F32)).astype(BF16)
            both = jnp.dot(jnp.concatenate([hi, lo], axis=0), perm, preferred_element_type=F32)
            al[rows, :, slot * 256 : slot * 256 + 256] = both.astype(BF16)

    def product(rows, n, first, depth):
        t = b[first : first + depth, cols(n)]
        hi = t.astype(BF16)
        lo = (t - hi.astype(F32)).astype(BF16)
        one = jnp.dot(al[rows, :, first : first + depth], hi, preferred_element_type=F32)
        two = jnp.dot(al[rows, 0:256, first : first + depth], lo, preferred_element_type=F32)
        return one[0:256] + (one[256:512] + two)

    def all_here(n, slots):
        for slot in slots:
            arrived(n, slot * 256 + (1 - core) * 128, 128, sib.at[n, slot])

    def c_copy(n):
        return pltpu.make_async_remote_copy(
            src_ref=c_out.at[n], dst_ref=o_ref.at[:, at(xlo * HALF + n * W, W, W)],
            send_sem=cs.at[n], recv_sem=cr.at[n], device_id=inner, device_id_type=MESH,
        )

    exchange(0)
    regroup(x_in, x_ref, lsem, tmp, stage, rest[:4], q, 1)
    regroup(x_in, x_ref, lsem, tmp, stage, rest[4:], q, 1)
    pieces = own_piece()
    for c in own_along_y() + pieces:
        c.start()
    load_a.wait()
    for c in a_x():
        c.start()
    regroup(x_in, x_ref, lsem, tmp, stage, rest[:4], q + 1, 7, False)
    exchange(1)
    regroup(x_in, x_ref, lsem, tmp, stage, rest[4:], q + 1, 7, False)
    for c in pieces:
        c.wait()

    def when(*conditions):
        ok = conditions[0]
        for c in conditions[1:]:
            ok = jnp.logical_and(ok, c)
        return pl.when(ok)

    @pl.loop(0, N + LAGC)
    def _(i):
        for g, (first, _, start) in enumerate(GROUPS):
            if start >= 0:
                @when(i == start)
                def _(g=g):
                    exchange(g)

            @when(i == first)
            def _(g=g):
                exchanged(g, ex)

        @when(i < N)
        def _():
            n = i
            push(n, mine(0) + 8, mine(1) + 8, 120, up, ty.at[n, 0])
            push(n, mine(0) + 8, mine(2) + 8, 120, down, ty.at[n, 1])

        @when(i == A_PAIR)
        def _():
            a_arrived(1, q, 0)
            a_arrived(1, qo, 1)
            for c in a_z(1, 3) + a_far():
                c.start()

        @when(i == A_OWN)
        def _():
            a_arrived(0, qo, 2)
            for c in a_z(0, 11):
                c.start()

        @when(i == A_PAIR + A_NEXT)
        def _():
            a_z_arrived(1, 3)
            for c in a_z_next(1, 3):
                c.start()

        @when(i == A_OWN + A_NEXT)
        def _():
            a_z_arrived(0, 11)
            for c in a_z_next(0, 11):
                c.start()

        @when(i == LAG2)
        def _():
            own_arrived()

        @when(i >= LAG2, i < N + LAG2)
        def _():
            n = i - LAG2
            arrived(n, mine(1) + 8, 120, ty.at[n, 0])
            push(n, mine(1), mine(3), 64, up, tf.at[n, 0])
            arrived(n, mine(2) + 8, 120, ty.at[n, 1])
            push(n, mine(2) + 64, mine(3) + 64, 64, down, tf.at[n, 1])
            for slot in range(3):
                push(n, mine(slot), mine(slot), 128, sibling, sib.at[n, slot])

        @when(i >= LAG3, i < N + LAG3)
        def _():
            n = i - LAG3
            arrived(n, mine(3), 64, tf.at[n, 0])
            arrived(n, mine(3) + 64, 64, tf.at[n, 1])
            push(n, mine(3), mine(3), 128, sibling, sib.at[n, 3])

        @when(i == LAGC)
        def _():
            a_z_all(1, 3)
            a_split(1)

        @when(i >= LAGC, i < LAGC + PAIRED)
        def _():
            n = i - LAGC
            all_here(n, range(4))
            c_out[n] = product(1, n, 0, 1024)
            c_copy(n).start()

        @when(i == LAGO)
        def _():
            a_z_all(0, 11)
            a_split(0)

        @when(i >= LAGO, i < LAGO + PAIRED)
        def _():
            n = i - LAGO
            o_ref[:, at(xlo * HALF + n * W, W, W)] = product(0, n, 0, 1024)

        @when(i >= LAGC + PAIRED)
        def _():
            n = i - LAGC
            all_here(n, range(3))
            part = product(0, n, 0, 768)
            all_here(n, (3,))
            o_ref[:, at(HALF + n * W, W, W)] = part + product(0, n, 768, 256)

    @pl.loop(0, PAIRED)
    def _(n):
        c = pltpu.make_async_copy(c_out.at[n], o_ref.at[:, at((1 - xlo) * HALF + n * W, W, W)], cr.at[n])
        c.wait()
        pltpu.make_async_copy(c_out.at[n], c_out.at[n], cs.at[n]).wait()

    @pl.loop(0, N)
    def _(n):
        sent = b.at[0:880, cols(n)]
        pltpu.make_async_copy(sent, sent, ssem.at[n]).wait()

    for g in range(len(GROUPS)):
        exchanged(g, exs)
    for c in own_along_y():
        c.wait_send()
    for c in a_x() + a_far() + a_z(1, 3) + a_z(0, 11) + a_z_next(1, 3) + a_z_next(0, 11):
        c.wait_send()


def write(c_ref, o_ref, sem):
    parts = [(c_ref.at[pl.ds(64 * i, 64)], o_ref.at[pl.ds(64 * i, 64)], sem.at[i]) for i in range(4)]
    for part in parts:
        pltpu.make_async_copy(*part).start()
    for part in parts:
        pltpu.make_async_copy(*part).wait()


def per_device(integrals, amplitudes):
    dma = pltpu.SemaphoreType.DMA
    anywhere = pl.BlockSpec(memory_space=pl.ANY)
    c = pl.pallas_call(
        kernel,
        name="cycle",
        out_shape=pltpu.VMEM((256, COLS), F32),
        in_specs=[anywhere, anywhere],
        out_specs=pl.BlockSpec(memory_space=pltpu.VMEM),
        scratch_shapes=[
            pltpu.VMEM((1024, N * W), F32),
            pltpu.VMEM((64, COLS), F32),
            pltpu.VMEM((5, 8, 8, 128), F32),
            pltpu.VMEM((2, 8, 256, 128), F32),
            pltpu.VMEM((2, 512, 1024), BF16),
            pltpu.VMEM((PAIRED, 256, W), F32),
            pltpu.VMEM((8, 80, 512), F32),
            dma((len(GROUPS),)),
            dma((len(GROUPS),)),
            dma((N, 2)),
            dma((N, 2)),
            dma((N, 4)),
            dma((PAIRED,)),
            dma((N,)),
            dma((PAIRED,)),
            dma((19,)),
            dma((19,)),
            dma((13,)),
            dma((4,)),
            dma((4,)),
        ],
        compiler_params=pltpu.CompilerParams(collective_id=0, has_side_effects=True, vmem_limit_bytes=52 << 20),
        cost_estimate=pl.CostEstimate(flops=3 * 2 * 256 * 1024 * COLS, bytes_accessed=7 << 20, transcendentals=0),
    )(integrals, amplitudes.reshape(8, 80, 512))
    return pl.pallas_call(
        write,
        name="write",
        out_shape=jax.ShapeDtypeStruct((256, COLS), F32),
        in_specs=[pl.BlockSpec(memory_space=pltpu.VMEM)],
        out_specs=anywhere,
        scratch_shapes=[dma((4,))],
        compiler_params=pltpu.CompilerParams(vmem_limit_bytes=8 << 20),
    )(c)


def solution(mesh):
    placed = (P("row", "col"), P("row", "col"))
    return jax.shard_map(
        per_device, mesh=mesh, in_specs=placed, out_specs=P("row", "col"), check_vma=False
    )
```

```python
import jax
import jax.numpy as jnp
from jax import lax
from jax.experimental import pallas as pl
from jax.experimental.pallas import tpu as pltpu
from jax.sharding import PartitionSpec as P

MESH = pl.DeviceIdType.MESH
F32, BF16 = jnp.float32, jnp.bfloat16
COLS = 5120
W = 256
PAIRED = 6
FULL = (COLS - 2 * PAIRED * W) // W
N = PAIRED + FULL
HALF = PAIRED * W
GROUPS = ((0, 1, -2), (1, 1, -1), (2, 2, 0), (4, 2, 1), (6, 4, 4), (10, 4, 7))
A_PAIR, A_OWN, A_NEXT = 2, 5, 2
FAR_FIRST = sorted(range(1, 16), key=lambda d: -(min(d // 2 % 4, 4 - d // 2 % 4) + (0, 2, 1, 1)[d // 8 * 2 + d % 2]))
LAG2, LAG3, LAGC, LAGO, LAGF = 2, 4, 6, 9, 5


def at(start, size, unit):
    return pl.ds(pl.multiple_of(start, unit), size)


def load(x_in, x_ref, lsem, g):
    rows = pl.ds(g * 8, 8)
    return pltpu.make_async_copy(x_in.at[:, rows], x_ref.at[:, rows], lsem.at[g])


def regroup(x_in, x_ref, lsem, tmp, stage, groups, first_q=0, count=8, wait=True):
    low = lax.broadcasted_iota(jnp.int32, (8, 128), 1) < 64
    for g in groups if wait else ():
        load(x_in, x_ref, lsem, g).wait()

    @pl.loop(0, count)
    def _(i):
        q = (first_q + i) % 8
        for slot, g in enumerate(groups):
            for t in range(4):
                v = x_ref[q, g * 8 : g * 8 + 8, t * 128 : (t + 1) * 128]
                nxt = pltpu.roll(v, 7, 0)
                tmp[slot, 2 * t] = jnp.where(low, v, pltpu.roll(nxt, 64, 1))
                tmp[slot, 2 * t + 1] = jnp.where(low, pltpu.roll(v, 64, 1), nxt)
            for u in range(4):
                col = (g * 4 + u) * 128
                stage[at(q * 8, 8, 8), col : col + 128] = tmp[slot, :, 2 * u, :]


def permutation(xlo, z, xhi):
    i = lax.broadcasted_iota(jnp.int32, (256, 256), 0)
    o = lax.broadcasted_iota(jnp.int32, (256, 256), 1)
    from_xlo = (xlo + (o >> 6)) & 1
    from_z = (z + 4 - ((o >> 4) & 3)) & 3
    from_xhi = (xhi + (o >> 3)) & 1
    source = from_xlo * 128 + ((o >> 7) & 1) * 64 + from_z * 16 + from_xhi * 8 + (o & 7)
    return (i == source).astype(F32).astype(BF16)


def kernel(a_in, x_in, o_ref, b, stage, tmp, ag, al, c_out, x_ref,
           ex, exs, ty, tf, sib, cr, ssem, cs, ar, asend, lsem, oy, oys):
    r, q = lax.axis_index("row"), lax.axis_index("col")
    xlo, y, core = r // 8, (r // 2) % 4, r % 2
    z, xhi = q // 2, q % 2

    def dev(xlo, y, core, z, xhi):
        return (xlo * 8 + y * 2 + core, z * 2 + xhi)

    up, down = dev(xlo, (y + 1) % 4, core, z, xhi), dev(xlo, (y + 3) % 4, core, z, xhi)
    inner = dev(1 - xlo, y, core, z, xhi)
    outer = dev(1 - xlo, y, core, z, 1 - xhi)
    sibling = dev(xlo, y, 1 - core, z, xhi)
    plane = []
    for d in FAR_FIRST:
        oxlo, oz, oxhi = (xlo + d // 8) % 2, (z + (d // 2) % 4) % 4, (xhi + d % 2) % 2
        plane.append((d, oxlo, oz * 2 + oxhi, dev(oxlo, y, core, oz, oxhi)))
    z_up, z_down = dev(xlo, y, core, (z + 1) % 4, xhi), dev(xlo, y, core, (z + 3) % 4, xhi)

    first = (0, HALF // 512)
    rest = tuple(g for g in range(COLS // 512) if g not in first)
    for g in first + rest:
        load(x_in, x_ref, lsem, g).start()
    load_a = pltpu.make_async_copy(a_in, ag.at[0, q], lsem.at[10])
    load_a.start()
    barrier = pltpu.get_barrier_semaphore()
    greeted = [p[3] for p in plane] + [up, down, sibling]
    for d in greeted:
        pl.semaphore_signal(barrier, inc=1, device_id=d, device_id_type=MESH)
    regroup(x_in, x_ref, lsem, tmp, stage, first)
    pl.semaphore_wait(barrier, len(greeted))

    def cols(n):
        return at(n * W, W, W)

    def push(n, src, dst, count, to, recv):
        pltpu.make_async_remote_copy(
            src_ref=b.at[at(src, count, 8), cols(n)], dst_ref=b.at[at(dst, count, 8), cols(n)],
            send_sem=ssem.at[n], recv_sem=recv, device_id=to, device_id_type=MESH,
        ).start()

    def arrived(n, row, count, recv):
        ref = b.at[at(row, count, 8), cols(n)]
        pltpu.make_async_copy(ref, ref, recv).wait()

    def mine(slot):
        return slot * 256 + core * 128

    def exchange(g):
        n, count, _ = GROUPS[g]
        for d, oxlo, oq, to in plane:
            first = at(oxlo * HALF + n * W, count * W, W) if n < PAIRED else pl.ds(HALF + n * W, count * W)
            pltpu.make_async_remote_copy(
                src_ref=stage.at[at(oq * 8, 8, 8), first],
                dst_ref=b.at[at(mine(0) + d * 8, 8, 8), pl.ds(n * W, count * W)],
                send_sem=exs.at[g], recv_sem=ex.at[g], device_id=to, device_id_type=MESH,
            ).start()

    def exchanged(g, sem):
        n, count, _ = GROUPS[g]
        ref = b.at[at(mine(0) + 8, 120, 8), pl.ds(n * W, count * W)]
        pltpu.make_async_copy(ref, ref, sem.at[g]).wait()

    parts = ((at(xlo * HALF, HALF, 128), pl.ds(0, HALF)), (pl.ds(2 * HALF, FULL * W), pl.ds(HALF, FULL * W)))

    def own_piece():
        src = at(q * 8, 8, 8)
        return [
            pltpu.make_async_copy(stage.at[src, frm], b.at[at(mine(0), 8, 8), to], lsem.at[11 + j])
            for j, (frm, to) in enumerate(parts)
        ]

    def own_along_y():
        src = at(q * 8, 8, 8)
        return [
            pltpu.make_async_remote_copy(
                src_ref=stage.at[src, frm], dst_ref=b.at[at(mine(1 + k), 8, 8), to],
                send_sem=oys.at[2 * j + k], recv_sem=oy.at[2 * j + k], device_id=d, device_id_type=MESH,
            )
            for j, (frm, to) in enumerate(parts) for k, d in enumerate((up, down))
        ]

    def own_arrived():
        for j, (_, to) in enumerate(parts):
            for k in range(2):
                ref = b.at[at(mine(1 + k), 8, 8), to]
                pltpu.make_async_copy(ref, ref, oy.at[2 * j + k]).wait()

    def a_push(rows, block, to_rows, i, to, part=pl.ds(0, 256)):
        return pltpu.make_async_remote_copy(
            src_ref=ag.at[rows, block, part], dst_ref=ag.at[to_rows, block, part],
            send_sem=asend.at[i], recv_sem=ar.at[i], device_id=to, device_id_type=MESH,
        )

    def a_arrived(rows, block, i, part=pl.ds(0, 256)):
        ref = ag.at[rows, block, part]
        pltpu.make_async_copy(ref, ref, ar.at[i]).wait()

    qo = z * 2 + 1 - xhi
    a_x = lambda: [a_push(0, q, 1, 0, inner), a_push(0, q, 1, 1, outer)]
    a_far = lambda: [a_push(1, q, 0, 2, outer)]
    top, bottom = pl.ds(0, 128), pl.ds(128, 128)

    def a_block(step, j):
        return ((z + step) % 4) * 2 + (xhi if j == 0 else 1 - xhi)

    def a_z(rows, i):
        return [
            a_push(rows, a_block(0, j), rows, i + 2 * j + k, to) for j in range(2) for k, to in enumerate((z_up, z_down))
        ]

    def a_z_next(rows, i):
        return [
            a_push(rows, a_block(3, j), rows, i + 4 + 2 * j, z_up, top) for j in range(2)
        ] + [
            a_push(rows, a_block(1, j), rows, i + 5 + 2 * j, z_down, bottom) for j in range(2)
        ]

    def a_z_arrived(rows, i):
        for j in range(2):
            a_arrived(rows, a_block(3, j), i + 2 * j)
            a_arrived(rows, a_block(1, j), i + 2 * j + 1)

    def a_z_all(rows, i):
        for j in range(2):
            a_arrived(rows, a_block(2, j), i + 4 + 2 * j, top)
            a_arrived(rows, a_block(2, j), i + 5 + 2 * j, bottom)

    def a_split(rows):
        perm = permutation(xlo, z, xhi)
        for slot, step in enumerate((0, 3, 1, 2)):
            yy = (y + step) % 4
            t = jnp.concatenate([ag[rows, yy], ag[rows, 4 + yy]], axis=1)
            hi = t.astype(BF16)
            lo = (t - hi.astype(F32)).astype(BF16)
            both = jnp.dot(jnp.concatenate([hi, lo], axis=0), perm, preferred_element_type=F32)
            al[rows, :, slot * 256 : slot * 256 + 256] = both.astype(BF16)

    def product(rows, n, first, depth):
        t = b[first : first + depth, cols(n)]
        hi = t.astype(BF16)
        lo = (t - hi.astype(F32)).astype(BF16)
        one = jnp.dot(al[rows, :, first : first + depth], hi, preferred_element_type=F32)
        two = jnp.dot(al[rows, 0:256, first : first + depth], lo, preferred_element_type=F32)
        return one[0:256] + (one[256:512] + two)

    def all_here(n, slots):
        for slot in slots:
            arrived(n, slot * 256 + (1 - core) * 128, 128, sib.at[n, slot])

    def c_copy(n):
        return pltpu.make_async_remote_copy(
            src_ref=c_out.at[n], dst_ref=o_ref.at[:, at(xlo * HALF + n * W, W, W)],
            send_sem=cs.at[n], recv_sem=cr.at[n], device_id=inner, device_id_type=MESH,
        )

    exchange(0)
    regroup(x_in, x_ref, lsem, tmp, stage, rest[:4], q, 1)
    regroup(x_in, x_ref, lsem, tmp, stage, rest[4:], q, 1)
    pieces = own_piece()
    for c in own_along_y() + pieces:
        c.start()
    load_a.wait()
    for c in a_x():
        c.start()
    regroup(x_in, x_ref, lsem, tmp, stage, rest[:4], q + 1, 7, False)
    exchange(1)
    regroup(x_in, x_ref, lsem, tmp, stage, rest[4:], q + 1, 7, False)
    for c in pieces:
        c.wait()

    def when(*conditions):
        ok = conditions[0]
        for c in conditions[1:]:
            ok = jnp.logical_and(ok, c)
        return pl.when(ok)

    @pl.loop(0, N + LAGF)
    def _(i):
        for g, (first, _, start) in enumerate(GROUPS):
            if start >= 0:
                @when(i == start)
                def _(g=g):
                    exchange(g)

            @when(i == first)
            def _(g=g):
                exchanged(g, ex)

        @when(i < N)
        def _():
            n = i
            push(n, mine(0) + 8, mine(1) + 8, 120, up, ty.at[n, 0])
            push(n, mine(0) + 8, mine(2) + 8, 120, down, ty.at[n, 1])

        @when(i == A_PAIR)
        def _():
            a_arrived(1, q, 0)
            a_arrived(1, qo, 1)
            for c in a_z(1, 3) + a_far():
                c.start()

        @when(i == A_OWN)
        def _():
            a_arrived(0, qo, 2)
            for c in a_z(0, 11):
                c.start()

        @when(i == A_PAIR + A_NEXT)
        def _():
            a_z_arrived(1, 3)
            for c in a_z_next(1, 3):
                c.start()

        @when(i == A_OWN + A_NEXT)
        def _():
            a_z_arrived(0, 11)
            for c in a_z_next(0, 11):
                c.start()

        @when(i == LAG2)
        def _():
            own_arrived()

        @when(i >= LAG2, i < N + LAG2)
        def _():
            n = i - LAG2
            arrived(n, mine(1) + 8, 120, ty.at[n, 0])
            push(n, mine(1), mine(3), 64, up, tf.at[n, 0])
            arrived(n, mine(2) + 8, 120, ty.at[n, 1])
            push(n, mine(2) + 64, mine(3) + 64, 64, down, tf.at[n, 1])
            for slot in range(3):
                push(n, mine(slot), mine(slot), 128, sibling, sib.at[n, slot])

        @when(i == LAGC)
        def _():
            a_z_all(1, 3)
            a_split(1)

        @when(i >= LAGC, i < LAGC + PAIRED)
        def _():
            n = i - LAGC
            all_here(n, range(4))
            c_out[n] = product(1, n, 0, 1024)
            c_copy(n).start()

        @when(i == LAGO)
        def _():
            a_z_all(0, 11)
            a_split(0)

        @when(i >= LAGO, i < LAGO + PAIRED)
        def _():
            n = i - LAGO
            o_ref[:, at(xlo * HALF + n * W, W, W)] = product(0, n, 0, 1024)

        @when(i >= LAGF + PAIRED)
        def _():
            n = i - LAGF
            all_here(n, range(3))
            part = product(0, n, 0, 768)
            all_here(n, (3,))
            o_ref[:, at(HALF + n * W, W, W)] = part + product(0, n, 768, 256)

        @when(i >= LAG3, i < N + LAG3)
        def _():
            n = i - LAG3
            arrived(n, mine(3), 64, tf.at[n, 0])
            arrived(n, mine(3) + 64, 64, tf.at[n, 1])
            push(n, mine(3), mine(3), 128, sibling, sib.at[n, 3])

    @pl.loop(0, PAIRED)
    def _(n):
        c = pltpu.make_async_copy(c_out.at[n], o_ref.at[:, at((1 - xlo) * HALF + n * W, W, W)], cr.at[n])
        c.wait()
        pltpu.make_async_copy(c_out.at[n], c_out.at[n], cs.at[n]).wait()

    @pl.loop(0, N)
    def _(n):
        sent = b.at[0:880, cols(n)]
        pltpu.make_async_copy(sent, sent, ssem.at[n]).wait()

    for g in range(len(GROUPS)):
        exchanged(g, exs)
    for c in own_along_y():
        c.wait_send()
    for c in a_x() + a_far() + a_z(1, 3) + a_z(0, 11) + a_z_next(1, 3) + a_z_next(0, 11):
        c.wait_send()


def write(c_ref, o_ref, sem):
    parts = [(c_ref.at[pl.ds(64 * i, 64)], o_ref.at[pl.ds(64 * i, 64)], sem.at[i]) for i in range(4)]
    for part in parts:
        pltpu.make_async_copy(*part).start()
    for part in parts:
        pltpu.make_async_copy(*part).wait()


def per_device(integrals, amplitudes):
    dma = pltpu.SemaphoreType.DMA
    anywhere = pl.BlockSpec(memory_space=pl.ANY)
    c = pl.pallas_call(
        kernel,
        name="cycle",
        out_shape=pltpu.VMEM((256, COLS), F32),
        in_specs=[anywhere, anywhere],
        out_specs=pl.BlockSpec(memory_space=pltpu.VMEM),
        scratch_shapes=[
            pltpu.VMEM((1024, N * W), F32),
            pltpu.VMEM((64, COLS), F32),
            pltpu.VMEM((5, 8, 8, 128), F32),
            pltpu.VMEM((2, 8, 256, 128), F32),
            pltpu.VMEM((2, 512, 1024), BF16),
            pltpu.VMEM((PAIRED, 256, W), F32),
            pltpu.VMEM((8, 80, 512), F32),
            dma((len(GROUPS),)),
            dma((len(GROUPS),)),
            dma((N, 2)),
            dma((N, 2)),
            dma((N, 4)),
            dma((PAIRED,)),
            dma((N,)),
            dma((PAIRED,)),
            dma((19,)),
            dma((19,)),
            dma((13,)),
            dma((4,)),
            dma((4,)),
        ],
        compiler_params=pltpu.CompilerParams(collective_id=0, has_side_effects=True, vmem_limit_bytes=52 << 20),
        cost_estimate=pl.CostEstimate(flops=3 * 2 * 256 * 1024 * COLS, bytes_accessed=7 << 20, transcendentals=0),
    )(integrals, amplitudes.reshape(8, 80, 512))
    return pl.pallas_call(
        write,
        name="write",
        out_shape=jax.ShapeDtypeStruct((256, COLS), F32),
        in_specs=[pl.BlockSpec(memory_space=pltpu.VMEM)],
        out_specs=anywhere,
        scratch_shapes=[dma((4,))],
        compiler_params=pltpu.CompilerParams(vmem_limit_bytes=8 << 20),
    )(c)


def solution(mesh):
    placed = (P("row", "col"), P("row", "col"))
    return jax.shard_map(
        per_device, mesh=mesh, in_specs=placed, out_specs=P("row", "col"), check_vma=False
    )
```

```python
import jax
import jax.numpy as jnp
from jax import lax
from jax.experimental import pallas as pl
from jax.experimental.pallas import tpu as pltpu
from jax.sharding import PartitionSpec as P

MESH = pl.DeviceIdType.MESH
F32, BF16 = jnp.float32, jnp.bfloat16
COLS = 5120
W = 256
PAIRED = 6
FULL = (COLS - 2 * PAIRED * W) // W
N = PAIRED + FULL
HALF = PAIRED * W
GROUPS = ((0, 1, -2), (1, 1, -1), (2, 2, 0), (4, 2, 1), (6, 2, 4), (8, 2, 5), (10, 2, 7), (12, 2, 8))
A_PAIR, A_OWN, A_NEXT = 2, 5, 2
FAR_FIRST = sorted(range(1, 16), key=lambda d: -(min(d // 2 % 4, 4 - d // 2 % 4) + (0, 2, 1, 1)[d // 8 * 2 + d % 2]))
LAG2, LAG3, LAGC, LAGO, LAGF = 2, 4, 6, 9, 5


def at(start, size, unit):
    return pl.ds(pl.multiple_of(start, unit), size)


def load(x_in, x_ref, lsem, g):
    rows = pl.ds(g * 8, 8)
    return pltpu.make_async_copy(x_in.at[:, rows], x_ref.at[:, rows], lsem.at[g])


def regroup(x_in, x_ref, lsem, tmp, stage, groups, first_q=0, count=8, wait=True):
    low = lax.broadcasted_iota(jnp.int32, (8, 128), 1) < 64
    for g in groups if wait else ():
        load(x_in, x_ref, lsem, g).wait()

    @pl.loop(0, count)
    def _(i):
        q = (first_q + i) % 8
        for slot, g in enumerate(groups):
            for t in range(4):
                v = x_ref[q, g * 8 : g * 8 + 8, t * 128 : (t + 1) * 128]
                nxt = pltpu.roll(v, 7, 0)
                tmp[slot, 2 * t] = jnp.where(low, v, pltpu.roll(nxt, 64, 1))
                tmp[slot, 2 * t + 1] = jnp.where(low, pltpu.roll(v, 64, 1), nxt)
            for u in range(4):
                col = (g * 4 + u) * 128
                stage[at(q * 8, 8, 8), col : col + 128] = tmp[slot, :, 2 * u, :]


def permutation(xlo, z, xhi):
    i = lax.broadcasted_iota(jnp.int32, (256, 256), 0)
    o = lax.broadcasted_iota(jnp.int32, (256, 256), 1)
    from_xlo = (xlo + (o >> 6)) & 1
    from_z = (z + 4 - ((o >> 4) & 3)) & 3
    from_xhi = (xhi + (o >> 3)) & 1
    source = from_xlo * 128 + ((o >> 7) & 1) * 64 + from_z * 16 + from_xhi * 8 + (o & 7)
    return (i == source).astype(F32).astype(BF16)


def kernel(a_in, x_in, o_ref, b, stage, tmp, ag, al, c_out, x_ref,
           ex, exs, ty, tf, sib, cr, ssem, cs, ar, asend, lsem, oy, oys):
    r, q = lax.axis_index("row"), lax.axis_index("col")
    xlo, y, core = r // 8, (r // 2) % 4, r % 2
    z, xhi = q // 2, q % 2

    def dev(xlo, y, core, z, xhi):
        return (xlo * 8 + y * 2 + core, z * 2 + xhi)

    up, down = dev(xlo, (y + 1) % 4, core, z, xhi), dev(xlo, (y + 3) % 4, core, z, xhi)
    inner = dev(1 - xlo, y, core, z, xhi)
    outer = dev(1 - xlo, y, core, z, 1 - xhi)
    sibling = dev(xlo, y, 1 - core, z, xhi)
    plane = []
    for d in FAR_FIRST:
        oxlo, oz, oxhi = (xlo + d // 8) % 2, (z + (d // 2) % 4) % 4, (xhi + d % 2) % 2
        plane.append((d, oxlo, oz * 2 + oxhi, dev(oxlo, y, core, oz, oxhi)))
    z_up, z_down = dev(xlo, y, core, (z + 1) % 4, xhi), dev(xlo, y, core, (z + 3) % 4, xhi)

    first = (0, HALF // 512)
    rest = tuple(g for g in range(COLS // 512) if g not in first)
    for g in first + rest:
        load(x_in, x_ref, lsem, g).start()
    load_a = pltpu.make_async_copy(a_in, ag.at[0, q], lsem.at[10])
    load_a.start()
    barrier = pltpu.get_barrier_semaphore()
    greeted = [p[3] for p in plane] + [up, down, sibling]
    for d in greeted:
        pl.semaphore_signal(barrier, inc=1, device_id=d, device_id_type=MESH)
    regroup(x_in, x_ref, lsem, tmp, stage, first)
    pl.semaphore_wait(barrier, len(greeted))

    def cols(n):
        return at(n * W, W, W)

    def push(n, src, dst, count, to, recv):
        pltpu.make_async_remote_copy(
            src_ref=b.at[at(src, count, 8), cols(n)], dst_ref=b.at[at(dst, count, 8), cols(n)],
            send_sem=ssem.at[n], recv_sem=recv, device_id=to, device_id_type=MESH,
        ).start()

    def arrived(n, row, count, recv):
        ref = b.at[at(row, count, 8), cols(n)]
        pltpu.make_async_copy(ref, ref, recv).wait()

    def mine(slot):
        return slot * 256 + core * 128

    def exchange(g):
        n, count, _ = GROUPS[g]
        for d, oxlo, oq, to in plane:
            first = at(oxlo * HALF + n * W, count * W, W) if n < PAIRED else pl.ds(HALF + n * W, count * W)
            pltpu.make_async_remote_copy(
                src_ref=stage.at[at(oq * 8, 8, 8), first],
                dst_ref=b.at[at(mine(0) + d * 8, 8, 8), pl.ds(n * W, count * W)],
                send_sem=exs.at[g], recv_sem=ex.at[g], device_id=to, device_id_type=MESH,
            ).start()

    def exchanged(g, sem):
        n, count, _ = GROUPS[g]
        ref = b.at[at(mine(0) + 8, 120, 8), pl.ds(n * W, count * W)]
        pltpu.make_async_copy(ref, ref, sem.at[g]).wait()

    parts = ((at(xlo * HALF, HALF, 128), pl.ds(0, HALF)), (pl.ds(2 * HALF, FULL * W), pl.ds(HALF, FULL * W)))

    def own_piece():
        src = at(q * 8, 8, 8)
        return [
            pltpu.make_async_copy(stage.at[src, frm], b.at[at(mine(0), 8, 8), to], lsem.at[11 + j])
            for j, (frm, to) in enumerate(parts)
        ]

    def own_along_y():
        src = at(q * 8, 8, 8)
        return [
            pltpu.make_async_remote_copy(
                src_ref=stage.at[src, frm], dst_ref=b.at[at(mine(1 + k), 8, 8), to],
                send_sem=oys.at[2 * j + k], recv_sem=oy.at[2 * j + k], device_id=d, device_id_type=MESH,
            )
            for j, (frm, to) in enumerate(parts) for k, d in enumerate((up, down))
        ]

    def own_arrived():
        for j, (_, to) in enumerate(parts):
            for k in range(2):
                ref = b.at[at(mine(1 + k), 8, 8), to]
                pltpu.make_async_copy(ref, ref, oy.at[2 * j + k]).wait()

    def a_push(rows, block, to_rows, i, to, part=pl.ds(0, 256)):
        return pltpu.make_async_remote_copy(
            src_ref=ag.at[rows, block, part], dst_ref=ag.at[to_rows, block, part],
            send_sem=asend.at[i], recv_sem=ar.at[i], device_id=to, device_id_type=MESH,
        )

    def a_arrived(rows, block, i, part=pl.ds(0, 256)):
        ref = ag.at[rows, block, part]
        pltpu.make_async_copy(ref, ref, ar.at[i]).wait()

    qo = z * 2 + 1 - xhi
    a_x = lambda: [a_push(0, q, 1, 0, inner), a_push(0, q, 1, 1, outer)]
    a_far = lambda: [a_push(1, q, 0, 2, outer)]
    top, bottom = pl.ds(0, 128), pl.ds(128, 128)

    def a_block(step, j):
        return ((z + step) % 4) * 2 + (xhi if j == 0 else 1 - xhi)

    def a_z(rows, i):
        return [
            a_push(rows, a_block(0, j), rows, i + 2 * j + k, to) for j in range(2) for k, to in enumerate((z_up, z_down))
        ]

    def a_z_next(rows, i):
        return [
            a_push(rows, a_block(3, j), rows, i + 4 + 2 * j, z_up, top) for j in range(2)
        ] + [
            a_push(rows, a_block(1, j), rows, i + 5 + 2 * j, z_down, bottom) for j in range(2)
        ]

    def a_z_arrived(rows, i):
        for j in range(2):
            a_arrived(rows, a_block(3, j), i + 2 * j)
            a_arrived(rows, a_block(1, j), i + 2 * j + 1)

    def a_z_all(rows, i):
        for j in range(2):
            a_arrived(rows, a_block(2, j), i + 4 + 2 * j, top)
            a_arrived(rows, a_block(2, j), i + 5 + 2 * j, bottom)

    def a_split(rows):
        perm = permutation(xlo, z, xhi)
        for slot, step in enumerate((0, 3, 1, 2)):
            yy = (y + step) % 4
            t = jnp.concatenate([ag[rows, yy], ag[rows, 4 + yy]], axis=1)
            hi = t.astype(BF16)
            lo = (t - hi.astype(F32)).astype(BF16)
            both = jnp.dot(jnp.concatenate([hi, lo], axis=0), perm, preferred_element_type=F32)
            al[rows, :, slot * 256 : slot * 256 + 256] = both.astype(BF16)

    def product(rows, n, first, depth):
        t = b[first : first + depth, cols(n)]
        hi = t.astype(BF16)
        lo = (t - hi.astype(F32)).astype(BF16)
        one = jnp.dot(al[rows, :, first : first + depth], hi, preferred_element_type=F32)
        two = jnp.dot(al[rows, 0:256, first : first + depth], lo, preferred_element_type=F32)
        return one[0:256] + (one[256:512] + two)

    def all_here(n, slots):
        for slot in slots:
            arrived(n, slot * 256 + (1 - core) * 128, 128, sib.at[n, slot])

    def c_copy(n):
        return pltpu.make_async_remote_copy(
            src_ref=c_out.at[n], dst_ref=o_ref.at[:, at(xlo * HALF + n * W, W, W)],
            send_sem=cs.at[n], recv_sem=cr.at[n], device_id=inner, device_id_type=MESH,
        )

    exchange(0)
    regroup(x_in, x_ref, lsem, tmp, stage, rest[:4], q, 1)
    regroup(x_in, x_ref, lsem, tmp, stage, rest[4:], q, 1)
    pieces = own_piece()
    for c in own_along_y() + pieces:
        c.start()
    load_a.wait()
    for c in a_x():
        c.start()
    regroup(x_in, x_ref, lsem, tmp, stage, rest[:4], q + 1, 7, False)
    exchange(1)
    regroup(x_in, x_ref, lsem, tmp, stage, rest[4:], q + 1, 7, False)
    for c in pieces:
        c.wait()

    def when(*conditions):
        ok = conditions[0]
        for c in conditions[1:]:
            ok = jnp.logical_and(ok, c)
        return pl.when(ok)

    @pl.loop(0, N + LAGF)
    def _(i):
        for g, (first, _, start) in enumerate(GROUPS):
            if start >= 0:
                @when(i == start)
                def _(g=g):
                    exchange(g)

            @when(i == first)
            def _(g=g):
                exchanged(g, ex)

        @when(i < N)
        def _():
            n = i
            push(n, mine(0) + 8, mine(1) + 8, 120, up, ty.at[n, 0])
            push(n, mine(0) + 8, mine(2) + 8, 120, down, ty.at[n, 1])

        @when(i == A_PAIR)
        def _():
            a_arrived(1, q, 0)
            a_arrived(1, qo, 1)
            for c in a_z(1, 3) + a_far():
                c.start()

        @when(i == A_OWN)
        def _():
            a_arrived(0, qo, 2)
            for c in a_z(0, 11):
                c.start()

        @when(i == A_PAIR + A_NEXT)
        def _():
            a_z_arrived(1, 3)
            for c in a_z_next(1, 3):
                c.start()

        @when(i == A_OWN + A_NEXT)
        def _():
            a_z_arrived(0, 11)
            for c in a_z_next(0, 11):
                c.start()

        @when(i == LAG2)
        def _():
            own_arrived()

        @when(i >= LAG2, i < N + LAG2)
        def _():
            n = i - LAG2
            arrived(n, mine(1) + 8, 120, ty.at[n, 0])
            push(n, mine(1), mine(3), 64, up, tf.at[n, 0])
            arrived(n, mine(2) + 8, 120, ty.at[n, 1])
            push(n, mine(2) + 64, mine(3) + 64, 64, down, tf.at[n, 1])
            for slot in range(3):
                push(n, mine(slot), mine(slot), 128, sibling, sib.at[n, slot])

        @when(i == LAGC)
        def _():
            a_z_all(1, 3)
            a_split(1)

        @when(i >= LAGC, i < LAGC + PAIRED)
        def _():
            n = i - LAGC
            all_here(n, range(4))
            c_out[n] = product(1, n, 0, 1024)
            c_copy(n).start()

        @when(i == LAGO)
        def _():
            a_z_all(0, 11)
            a_split(0)

        @when(i >= LAGO, i < LAGO + PAIRED)
        def _():
            n = i - LAGO
            o_ref[:, at(xlo * HALF + n * W, W, W)] = product(0, n, 0, 1024)

        @when(i >= LAGF + PAIRED)
        def _():
            n = i - LAGF
            all_here(n, range(3))
            part = product(0, n, 0, 768)
            all_here(n, (3,))
            o_ref[:, at(HALF + n * W, W, W)] = part + product(0, n, 768, 256)

        @when(i >= LAG3, i < N + LAG3)
        def _():
            n = i - LAG3
            arrived(n, mine(3), 64, tf.at[n, 0])
            arrived(n, mine(3) + 64, 64, tf.at[n, 1])
            push(n, mine(3), mine(3), 128, sibling, sib.at[n, 3])

    @pl.loop(0, PAIRED)
    def _(n):
        c = pltpu.make_async_copy(c_out.at[n], o_ref.at[:, at((1 - xlo) * HALF + n * W, W, W)], cr.at[n])
        c.wait()
        pltpu.make_async_copy(c_out.at[n], c_out.at[n], cs.at[n]).wait()

    @pl.loop(0, N)
    def _(n):
        sent = b.at[0:880, cols(n)]
        pltpu.make_async_copy(sent, sent, ssem.at[n]).wait()

    for g in range(len(GROUPS)):
        exchanged(g, exs)
    for c in own_along_y():
        c.wait_send()
    for c in a_x() + a_far() + a_z(1, 3) + a_z(0, 11) + a_z_next(1, 3) + a_z_next(0, 11):
        c.wait_send()


def write(c_ref, o_ref, sem):
    parts = [(c_ref.at[pl.ds(64 * i, 64)], o_ref.at[pl.ds(64 * i, 64)], sem.at[i]) for i in range(4)]
    for part in parts:
        pltpu.make_async_copy(*part).start()
    for part in parts:
        pltpu.make_async_copy(*part).wait()


def per_device(integrals, amplitudes):
    dma = pltpu.SemaphoreType.DMA
    anywhere = pl.BlockSpec(memory_space=pl.ANY)
    c = pl.pallas_call(
        kernel,
        name="cycle",
        out_shape=pltpu.VMEM((256, COLS), F32),
        in_specs=[anywhere, anywhere],
        out_specs=pl.BlockSpec(memory_space=pltpu.VMEM),
        scratch_shapes=[
            pltpu.VMEM((1024, N * W), F32),
            pltpu.VMEM((64, COLS), F32),
            pltpu.VMEM((5, 8, 8, 128), F32),
            pltpu.VMEM((2, 8, 256, 128), F32),
            pltpu.VMEM((2, 512, 1024), BF16),
            pltpu.VMEM((PAIRED, 256, W), F32),
            pltpu.VMEM((8, 80, 512), F32),
            dma((len(GROUPS),)),
            dma((len(GROUPS),)),
            dma((N, 2)),
            dma((N, 2)),
            dma((N, 4)),
            dma((PAIRED,)),
            dma((N,)),
            dma((PAIRED,)),
            dma((19,)),
            dma((19,)),
            dma((13,)),
            dma((4,)),
            dma((4,)),
        ],
        compiler_params=pltpu.CompilerParams(collective_id=0, has_side_effects=True, vmem_limit_bytes=52 << 20),
        cost_estimate=pl.CostEstimate(flops=3 * 2 * 256 * 1024 * COLS, bytes_accessed=7 << 20, transcendentals=0),
    )(integrals, amplitudes.reshape(8, 80, 512))
    return pl.pallas_call(
        write,
        name="write",
        out_shape=jax.ShapeDtypeStruct((256, COLS), F32),
        in_specs=[pl.BlockSpec(memory_space=pltpu.VMEM)],
        out_specs=anywhere,
        scratch_shapes=[dma((4,))],
        compiler_params=pltpu.CompilerParams(vmem_limit_bytes=8 << 20),
    )(c)


def solution(mesh):
    placed = (P("row", "col"), P("row", "col"))
    return jax.shard_map(
        per_device, mesh=mesh, in_specs=placed, out_specs=P("row", "col"), check_vma=False
    )
```

```python
import jax
import jax.numpy as jnp
from jax import lax
from jax.experimental import pallas as pl
from jax.experimental.pallas import tpu as pltpu
from jax.sharding import PartitionSpec as P

MESH = pl.DeviceIdType.MESH
F32, BF16 = jnp.float32, jnp.bfloat16
COLS = 5120
W = 256
PAIRED = 6
FULL = (COLS - 2 * PAIRED * W) // W
N = PAIRED + FULL
HALF = PAIRED * W
GROUPS = ((0, 1, -2), (1, 1, -1), (2, 2, 0), (4, 2, 1), (6, 2, 4), (8, 2, 5), (10, 2, 7), (12, 2, 8))
A_PAIR, A_OWN, A_NEXT = 2, 5, 2
FAR_FIRST = sorted(range(1, 16), key=lambda d: -(min(d // 2 % 4, 4 - d // 2 % 4) + (0, 2, 1, 1)[d // 8 * 2 + d % 2]))
LAG2, LAG3, LAGC, LAGO, LAGF = 2, 4, 6, 9, 5


def at(start, size, unit):
    return pl.ds(pl.multiple_of(start, unit), size)


def load(x_in, x_ref, lsem, g):
    rows = pl.ds(g * 8, 8)
    return pltpu.make_async_copy(x_in.at[:, rows], x_ref.at[:, rows], lsem.at[g])


def regroup(x_in, x_ref, lsem, tmp, stage, groups, first_q=0, count=8, wait=True):
    low = lax.broadcasted_iota(jnp.int32, (8, 128), 1) < 64
    for g in groups if wait else ():
        load(x_in, x_ref, lsem, g).wait()

    @pl.loop(0, count)
    def _(i):
        q = (first_q + i) % 8
        for slot, g in enumerate(groups):
            for t in range(4):
                v = x_ref[q, g * 8 : g * 8 + 8, t * 128 : (t + 1) * 128]
                nxt = pltpu.roll(v, 7, 0)
                tmp[slot, 2 * t] = jnp.where(low, v, pltpu.roll(nxt, 64, 1))
                tmp[slot, 2 * t + 1] = jnp.where(low, pltpu.roll(v, 64, 1), nxt)
            for u in range(4):
                col = (g * 4 + u) * 128
                stage[at(q * 8, 8, 8), col : col + 128] = tmp[slot, :, 2 * u, :]


def permutation(xlo, z, xhi):
    i = lax.broadcasted_iota(jnp.int32, (256, 256), 0)
    o = lax.broadcasted_iota(jnp.int32, (256, 256), 1)
    from_xlo = (xlo + (o >> 6)) & 1
    from_z = (z + 4 - ((o >> 4) & 3)) & 3
    from_xhi = (xhi + (o >> 3)) & 1
    source = from_xlo * 128 + ((o >> 7) & 1) * 64 + from_z * 16 + from_xhi * 8 + (o & 7)
    return (i == source).astype(F32).astype(BF16)


def kernel(a_in, x_in, o_ref, b, stage, tmp, ag, al, c_out, x_ref,
           ex, exs, ty, tf, sib, cr, ssem, cs, ar, asend, lsem, oy, oys):
    r, q = lax.axis_index("row"), lax.axis_index("col")
    xlo, y, core = r // 8, (r // 2) % 4, r % 2
    z, xhi = q // 2, q % 2

    def dev(xlo, y, core, z, xhi):
        return (xlo * 8 + y * 2 + core, z * 2 + xhi)

    up, down = dev(xlo, (y + 1) % 4, core, z, xhi), dev(xlo, (y + 3) % 4, core, z, xhi)
    inner = dev(1 - xlo, y, core, z, xhi)
    outer = dev(1 - xlo, y, core, z, 1 - xhi)
    sibling = dev(xlo, y, 1 - core, z, xhi)
    plane = []
    for d in FAR_FIRST:
        oxlo, oz, oxhi = (xlo + d // 8) % 2, (z + (d // 2) % 4) % 4, (xhi + d % 2) % 2
        plane.append((d, oxlo, oz * 2 + oxhi, dev(oxlo, y, core, oz, oxhi)))
    z_up, z_down = dev(xlo, y, core, (z + 1) % 4, xhi), dev(xlo, y, core, (z + 3) % 4, xhi)

    first = (0, HALF // 512)
    rest = tuple(g for g in range(COLS // 512) if g not in first)
    for g in first + rest:
        load(x_in, x_ref, lsem, g).start()
    load_a = pltpu.make_async_copy(a_in, ag.at[0, q], lsem.at[10])
    load_a.start()
    barrier = pltpu.get_barrier_semaphore()
    greeted = [p[3] for p in plane] + [up, down, sibling]
    for d in greeted:
        pl.semaphore_signal(barrier, inc=1, device_id=d, device_id_type=MESH)
    regroup(x_in, x_ref, lsem, tmp, stage, first)
    pl.semaphore_wait(barrier, len(greeted))

    def cols(n):
        return at(n * W, W, W)

    def push(n, src, dst, count, to, recv):
        pltpu.make_async_remote_copy(
            src_ref=b.at[at(src, count, 8), cols(n)], dst_ref=b.at[at(dst, count, 8), cols(n)],
            send_sem=ssem.at[n], recv_sem=recv, device_id=to, device_id_type=MESH,
        ).start()

    def arrived(n, row, count, recv):
        ref = b.at[at(row, count, 8), cols(n)]
        pltpu.make_async_copy(ref, ref, recv).wait()

    def mine(slot):
        return slot * 256 + core * 128

    def exchange(g):
        n, count, _ = GROUPS[g]
        for d, oxlo, oq, to in plane:
            first = at(oxlo * HALF + n * W, count * W, W) if n < PAIRED else pl.ds(HALF + n * W, count * W)
            pltpu.make_async_remote_copy(
                src_ref=stage.at[at(oq * 8, 8, 8), first],
                dst_ref=b.at[at(mine(0) + d * 8, 8, 8), pl.ds(n * W, count * W)],
                send_sem=exs.at[g], recv_sem=ex.at[g], device_id=to, device_id_type=MESH,
            ).start()

    def exchanged(g, sem):
        n, count, _ = GROUPS[g]
        ref = b.at[at(mine(0) + 8, 120, 8), pl.ds(n * W, count * W)]
        pltpu.make_async_copy(ref, ref, sem.at[g]).wait()

    parts = ((at(xlo * HALF, HALF, 128), pl.ds(0, HALF)), (pl.ds(2 * HALF, FULL * W), pl.ds(HALF, FULL * W)))

    def own_piece():
        src = at(q * 8, 8, 8)
        return [
            pltpu.make_async_copy(stage.at[src, frm], b.at[at(mine(0), 8, 8), to], lsem.at[11 + j])
            for j, (frm, to) in enumerate(parts)
        ]

    def own_along_y():
        src = at(q * 8, 8, 8)
        return [
            pltpu.make_async_remote_copy(
                src_ref=stage.at[src, frm], dst_ref=b.at[at(mine(1 + k), 8, 8), to],
                send_sem=oys.at[2 * j + k], recv_sem=oy.at[2 * j + k], device_id=d, device_id_type=MESH,
            )
            for j, (frm, to) in enumerate(parts) for k, d in enumerate((up, down))
        ]

    def own_arrived():
        for j, (_, to) in enumerate(parts):
            for k in range(2):
                ref = b.at[at(mine(1 + k), 8, 8), to]
                pltpu.make_async_copy(ref, ref, oy.at[2 * j + k]).wait()

    def a_push(rows, block, to_rows, i, to, part=pl.ds(0, 256)):
        return pltpu.make_async_remote_copy(
            src_ref=ag.at[rows, block, part], dst_ref=ag.at[to_rows, block, part],
            send_sem=asend.at[i], recv_sem=ar.at[i], device_id=to, device_id_type=MESH,
        )

    def a_arrived(rows, block, i, part=pl.ds(0, 256)):
        ref = ag.at[rows, block, part]
        pltpu.make_async_copy(ref, ref, ar.at[i]).wait()

    qo = z * 2 + 1 - xhi
    a_x = lambda: [a_push(0, q, 1, 0, inner), a_push(0, q, 1, 1, outer)]
    a_far = lambda: [a_push(1, q, 0, 2, outer)]
    top, bottom = pl.ds(0, 128), pl.ds(128, 128)

    def a_block(step, j):
        return ((z + step) % 4) * 2 + (xhi if j == 0 else 1 - xhi)

    def a_z(rows, i):
        return [
            a_push(rows, a_block(0, j), rows, i + 2 * j + k, to) for j in range(2) for k, to in enumerate((z_up, z_down))
        ]

    def a_z_next(rows, i):
        return [
            a_push(rows, a_block(3, j), rows, i + 4 + 2 * j, z_up, top) for j in range(2)
        ] + [
            a_push(rows, a_block(1, j), rows, i + 5 + 2 * j, z_down, bottom) for j in range(2)
        ]

    def a_z_arrived(rows, i):
        for j in range(2):
            a_arrived(rows, a_block(3, j), i + 2 * j)
            a_arrived(rows, a_block(1, j), i + 2 * j + 1)

    def a_z_all(rows, i):
        for j in range(2):
            a_arrived(rows, a_block(2, j), i + 4 + 2 * j, top)
            a_arrived(rows, a_block(2, j), i + 5 + 2 * j, bottom)

    def a_split(rows):
        perm = permutation(xlo, z, xhi)
        for slot, step in enumerate((0, 3, 1, 2)):
            yy = (y + step) % 4
            t = jnp.concatenate([ag[rows, yy], ag[rows, 4 + yy]], axis=1)
            hi = t.astype(BF16)
            lo = (t - hi.astype(F32)).astype(BF16)
            both = jnp.dot(jnp.concatenate([hi, lo], axis=0), perm, preferred_element_type=F32)
            al[rows, :, slot * 256 : slot * 256 + 256] = both.astype(BF16)

    def product(rows, n, first, depth):
        t = b[first : first + depth, cols(n)]
        hi = t.astype(BF16)
        lo = (t - hi.astype(F32)).astype(BF16)
        one = jnp.dot(al[rows, :, first : first + depth], hi, preferred_element_type=F32)
        two = jnp.dot(al[rows, 0:256, first : first + depth], lo, preferred_element_type=F32)
        return one[0:256] + (one[256:512] + two)

    def all_here(n, slots):
        for slot in slots:
            arrived(n, slot * 256 + (1 - core) * 128, 128, sib.at[n, slot])

    def c_copy(n):
        return pltpu.make_async_remote_copy(
            src_ref=c_out.at[n], dst_ref=o_ref.at[:, at(xlo * HALF + n * W, W, W)],
            send_sem=cs.at[n], recv_sem=cr.at[n], device_id=inner, device_id_type=MESH,
        )

    exchange(0)
    regroup(x_in, x_ref, lsem, tmp, stage, rest[:4], q, 1)
    regroup(x_in, x_ref, lsem, tmp, stage, rest[4:], q, 1)
    pieces = own_piece()
    for c in own_along_y() + pieces:
        c.start()
    load_a.wait()
    for c in a_x():
        c.start()
    regroup(x_in, x_ref, lsem, tmp, stage, rest[:4], q + 1, 7, False)
    exchange(1)
    regroup(x_in, x_ref, lsem, tmp, stage, rest[4:], q + 1, 7, False)
    for c in pieces:
        c.wait()

    def when(*conditions):
        ok = conditions[0]
        for c in conditions[1:]:
            ok = jnp.logical_and(ok, c)
        return pl.when(ok)

    @pl.loop(0, N + LAGF)
    def _(i):
        for g, (first, _, start) in enumerate(GROUPS):
            if start >= 0:
                @when(i == start)
                def _(g=g):
                    exchange(g)

            @when(i == first)
            def _(g=g):
                exchanged(g, ex)

        @when(i < N)
        def _():
            n = i
            push(n, mine(0) + 8, mine(1) + 8, 120, up, ty.at[n, 0])
            push(n, mine(0) + 8, mine(2) + 8, 120, down, ty.at[n, 1])
            push(n, mine(0), mine(0), 128, sibling, sib.at[n, 0])

        @when(i == A_PAIR)
        def _():
            a_arrived(1, q, 0)
            a_arrived(1, qo, 1)
            for c in a_z(1, 3) + a_far():
                c.start()

        @when(i == A_OWN)
        def _():
            a_arrived(0, qo, 2)
            for c in a_z(0, 11):
                c.start()

        @when(i == A_PAIR + A_NEXT)
        def _():
            a_z_arrived(1, 3)
            for c in a_z_next(1, 3):
                c.start()

        @when(i == A_OWN + A_NEXT)
        def _():
            a_z_arrived(0, 11)
            for c in a_z_next(0, 11):
                c.start()

        @when(i == LAG2)
        def _():
            own_arrived()

        @when(i >= LAG2, i < N + LAG2)
        def _():
            n = i - LAG2
            arrived(n, mine(1) + 8, 120, ty.at[n, 0])
            push(n, mine(1), mine(3), 64, up, tf.at[n, 0])
            arrived(n, mine(2) + 8, 120, ty.at[n, 1])
            push(n, mine(2) + 64, mine(3) + 64, 64, down, tf.at[n, 1])
            for slot in (1, 2):
                push(n, mine(slot), mine(slot), 128, sibling, sib.at[n, slot])

        @when(i == LAGC)
        def _():
            a_z_all(1, 3)
            a_split(1)

        @when(i >= LAGC, i < LAGC + PAIRED)
        def _():
            n = i - LAGC
            all_here(n, range(4))
            c_out[n] = product(1, n, 0, 1024)
            c_copy(n).start()

        @when(i == LAGO)
        def _():
            a_z_all(0, 11)
            a_split(0)

        @when(i >= LAGO, i < LAGO + PAIRED)
        def _():
            n = i - LAGO
            o_ref[:, at(xlo * HALF + n * W, W, W)] = product(0, n, 0, 1024)

        @when(i >= LAGF + PAIRED)
        def _():
            n = i - LAGF
            all_here(n, range(3))
            part = product(0, n, 0, 768)
            all_here(n, (3,))
            o_ref[:, at(HALF + n * W, W, W)] = part + product(0, n, 768, 256)

        @when(i >= LAG3, i < N + LAG3)
        def _():
            n = i - LAG3
            arrived(n, mine(3), 64, tf.at[n, 0])
            arrived(n, mine(3) + 64, 64, tf.at[n, 1])
            push(n, mine(3), mine(3), 128, sibling, sib.at[n, 3])

    @pl.loop(0, PAIRED)
    def _(n):
        c = pltpu.make_async_copy(c_out.at[n], o_ref.at[:, at((1 - xlo) * HALF + n * W, W, W)], cr.at[n])
        c.wait()
        pltpu.make_async_copy(c_out.at[n], c_out.at[n], cs.at[n]).wait()

    @pl.loop(0, N)
    def _(n):
        sent = b.at[0:880, cols(n)]
        pltpu.make_async_copy(sent, sent, ssem.at[n]).wait()

    for g in range(len(GROUPS)):
        exchanged(g, exs)
    for c in own_along_y():
        c.wait_send()
    for c in a_x() + a_far() + a_z(1, 3) + a_z(0, 11) + a_z_next(1, 3) + a_z_next(0, 11):
        c.wait_send()


def write(c_ref, o_ref, sem):
    parts = [(c_ref.at[pl.ds(64 * i, 64)], o_ref.at[pl.ds(64 * i, 64)], sem.at[i]) for i in range(4)]
    for part in parts:
        pltpu.make_async_copy(*part).start()
    for part in parts:
        pltpu.make_async_copy(*part).wait()


def per_device(integrals, amplitudes):
    dma = pltpu.SemaphoreType.DMA
    anywhere = pl.BlockSpec(memory_space=pl.ANY)
    c = pl.pallas_call(
        kernel,
        name="cycle",
        out_shape=pltpu.VMEM((256, COLS), F32),
        in_specs=[anywhere, anywhere],
        out_specs=pl.BlockSpec(memory_space=pltpu.VMEM),
        scratch_shapes=[
            pltpu.VMEM((1024, N * W), F32),
            pltpu.VMEM((64, COLS), F32),
            pltpu.VMEM((5, 8, 8, 128), F32),
            pltpu.VMEM((2, 8, 256, 128), F32),
            pltpu.VMEM((2, 512, 1024), BF16),
            pltpu.VMEM((PAIRED, 256, W), F32),
            pltpu.VMEM((8, 80, 512), F32),
            dma((len(GROUPS),)),
            dma((len(GROUPS),)),
            dma((N, 2)),
            dma((N, 2)),
            dma((N, 4)),
            dma((PAIRED,)),
            dma((N,)),
            dma((PAIRED,)),
            dma((19,)),
            dma((19,)),
            dma((13,)),
            dma((4,)),
            dma((4,)),
        ],
        compiler_params=pltpu.CompilerParams(collective_id=0, has_side_effects=True, vmem_limit_bytes=52 << 20),
        cost_estimate=pl.CostEstimate(flops=3 * 2 * 256 * 1024 * COLS, bytes_accessed=7 << 20, transcendentals=0),
    )(integrals, amplitudes.reshape(8, 80, 512))
    return pl.pallas_call(
        write,
        name="write",
        out_shape=jax.ShapeDtypeStruct((256, COLS), F32),
        in_specs=[pl.BlockSpec(memory_space=pltpu.VMEM)],
        out_specs=anywhere,
        scratch_shapes=[dma((4,))],
        compiler_params=pltpu.CompilerParams(vmem_limit_bytes=8 << 20),
    )(c)


def solution(mesh):
    placed = (P("row", "col"), P("row", "col"))
    return jax.shard_map(
        per_device, mesh=mesh, in_specs=placed, out_specs=P("row", "col"), check_vma=False
    )
```
